1024 devices in a mesh: atoms: 64 (over y, z), space: 16 (over x, core).
Axes of the slice: x: 8, y: 8, z: 8, core: 2. Of those that a mesh axis runs over, the one named last changes fastest.
Arguments:
- block_store: bfloat16 [16, 256, 128, 128], P('space', 'atoms'), may hold values from -0.21875 to 0.21875
- block_source: int32 [64, 16, 36], P('atoms', 'space'), may hold values from 0 to 255, as said below
- chem_pot: float32 [1], replicated, may hold values from -0.6 to 0.6
- basis_values: bfloat16 [64, 16, 8, 128, 1024], P('atoms', 'space'), may hold values from -1.5 to 1.5
- core_density: float32 [64, 16, 1024], P('atoms', 'space'), may hold values from 0.5 to 4
- point_weights: float32 [64, 16, 1024], P('atoms', 'space'), may hold values from 0.2 to 0.8
- pair_dest: int32 [64, 16, 12], P('atoms', 'space'), may hold values from 0 to 15, as said below
- tile_pairs: int32 [64, 16, 2, 16], P('atoms', 'space'), may hold values from -1 to 7, as said below
Outputs:
- density: bfloat16 [64, 16, 768, 128], P('atoms', 'space')
- potential: float32 [64, 16, 1024], P('atoms', 'space')
- kohn_sham: float32 [64, 16, 768, 128], P('atoms', 'space')
The draws below stay inside these ranges and needn't reach their ends.
Inputs may be any that keep to these rules, and one draw needn't show every extreme that they name: `block_source`: each device names at most 1 block whose number // 4 is the same; blocks may repeat. `pair_dest`: the two pairs of one density block go to different tiles; a device sends at most 1 pairs to one tile. `tile_pairs`: slots that receive no pair hold -1 in both entries; the others follow the pairs as stated.
All inputs are finite; a program needn't handle non-finite values.
Results may differ from the reference program's by a relative error of at most 0.0065.
Values may be sent and summed in bfloat16 or wider, within the bound.
A program may use at most 32 MiB of HBM per device.

```python
import math
import jax
import jax.numpy as jnp
from jax import lax

B = 128
KB = 6
M = 768
SLOTS = 36
SENDS = 12
NB_DEV = 4
NLOC = 8
PTS = 1024
CAPT = 1
N_ATOMS = 64
N_SPACE = 16


def draw_block_source(key, part):
    device_keys = jax.random.split(key, N_ATOMS * N_SPACE)
    atom_ids = jnp.arange(N_ATOMS * N_SPACE) // N_SPACE

    def single(one_key, atom_id):
        first_key, second_key = jax.random.split(one_key)
        shuffled = jax.random.permutation(first_key, N_ATOMS).astype(jnp.int32)
        target = jnp.where(atom_id == 0, N_ATOMS - 1, jnp.where(atom_id == N_ATOMS - 1, 0, shuffled[0]))
        swapped = jnp.where(shuffled == target, shuffled[0], shuffled)
        swapped = swapped.at[0].set(target)
        peers = swapped[jnp.arange(SLOTS) % N_ATOMS]
        chosen = jax.random.randint(second_key, (SLOTS,), 0, NB_DEV)
        forced = jnp.where(atom_id == 0, NB_DEV - 1, jnp.where(atom_id == N_ATOMS - 1, 0, chosen[0]))
        chosen = chosen.at[0].set(forced)
        return (peers * NB_DEV + chosen).astype(jnp.int32)
    return jax.vmap(single)(device_keys, atom_ids).reshape(N_ATOMS, N_SPACE, SLOTS)


def pair_tables(key):
    base_key = jax.random.fold_in(key, 811)

    def group(atom_id):
        group_key = jax.random.fold_in(base_key, atom_id)
        order_keys = jax.random.split(jax.random.fold_in(group_key, 1), N_SPACE)
        orders = jax.vmap(lambda one_key: jax.random.permutation(one_key, N_SPACE))(order_keys).astype(jnp.int32)
        sends = jnp.arange(SENDS)
        destinations = orders[:, sends % N_SPACE]
        arrival = sends // N_SPACE
        row_blocks = jax.random.randint(jax.random.fold_in(group_key, 2), (N_SPACE, SENDS), 0, NLOC)
        col_blocks = jax.random.randint(jax.random.fold_in(group_key, 3), (N_SPACE, SENDS), 0, NLOC)
        row_blocks = row_blocks.at[0, 0].set(jnp.where(atom_id == 0, NLOC - 1, row_blocks[0, 0]))
        slot_at = jnp.arange(N_SPACE)[:, None] * CAPT + arrival[None, :]
        table = jnp.full((N_SPACE, 2, N_SPACE * CAPT), -1, jnp.int32)
        table = table.at[destinations, 0, slot_at].set(row_blocks.astype(jnp.int32))
        table = table.at[destinations, 1, slot_at].set(col_blocks.astype(jnp.int32))
        return (destinations.astype(jnp.int32), table)
    return jax.vmap(group)(jnp.arange(N_ATOMS))


def draw_pair_dest(key, part):
    return pair_tables(key)[0]


def draw_tile_pairs(key, part):
    return pair_tables(key)[1]


def block_levels(own_key, shape, pieces, least, high):
    level = 1.0
    for dim, blocks in pieces:
        heights = jax.random.uniform(jax.random.fold_in(jax.random.fold_in(own_key, 6), dim), (blocks,), jnp.float32, least / len(pieces), high / len(pieces))
        level = level * jnp.repeat(jnp.exp(heights), shape[dim] // blocks).reshape((-1,) + (1,) * (len(shape) - 1 - dim))
    return level


def noise(key, extent, spread, most, cuts=(), kind=jnp.bfloat16):
    loudness = block_levels(key, extent, cuts, -0.22, 0.18) if cuts else 1.0
    values = jax.random.normal(key, extent, jnp.float32) * spread * loudness
    return jnp.minimum(jnp.maximum(values, -most), most).astype(kind)


def setup_inputs(seed: int = 0) -> dict:
    splits = jax.random.split(jax.random.key(seed), 9)
    block_store = noise(splits[0], (N_SPACE, N_ATOMS * NB_DEV, B, B), M ** -0.5, 0.21875, ((0, 16), (1, 64)))
    block_source = draw_block_source(jax.random.fold_in(splits[8], 71), 0)
    chem_pot = jnp.clip(jax.random.uniform(splits[2], (1,), jnp.float32, -0.6, 0.6), -0.6, 0.6)
    basis_values = noise(splits[3], (N_ATOMS, N_SPACE, NLOC, B, PTS), 0.25, 1.5, ((0, 64), (1, 16)))
    core_density = jnp.clip(jnp.exp(math.log(4.0) - 2.0794415 * jax.random.uniform(splits[4], (N_ATOMS, N_SPACE, PTS), jnp.float32) ** block_levels(splits[4], (N_ATOMS, N_SPACE, PTS), ((0, 64), (1, 16)), -0.2, 0.2)), 0.5, 4.0)
    point_weights = jnp.clip(0.2 + 0.6 * jax.random.uniform(splits[5], (N_ATOMS, N_SPACE, PTS), jnp.float32) ** block_levels(splits[5], (N_ATOMS, N_SPACE, PTS), ((0, 64), (1, 16)), -0.2, 0.2), 0.2, 0.8)
    pair_dest = draw_pair_dest(jax.random.fold_in(splits[8], 71), 0)
    tile_pairs = draw_tile_pairs(jax.random.fold_in(splits[8], 71), 0)
    return {"block_store": block_store, "block_source": block_source, "chem_pot": chem_pot, "basis_values": basis_values, "core_density": core_density, "point_weights": point_weights, "pair_dest": pair_dest, "tile_pairs": tile_pairs}


slater_factor = math.pow(3.0 / math.pi, 1.0 / 3.0)
density_floor = 0.05

def sign_density(blocks, chem):
    matrix = blocks.reshape(KB, KB, B, B).transpose(0, 2, 1, 3).reshape(M, M)
    widened = matrix.astype(jnp.float32)
    identity = jnp.eye(M, dtype=jnp.float32)
    shifted = 0.5 * (widened + widened.T) - chem * identity
    scaling = 2.0 * jnp.sqrt(jnp.sum(shifted * shifted) / M + 1e-06)
    start_x = (shifted / scaling).astype(jnp.bfloat16)
    square_one = jnp.dot(start_x, start_x, preferred_element_type=jnp.float32)
    factor_one = (1.5 * identity - 0.5 * square_one).astype(jnp.bfloat16)
    next_x = jnp.dot(start_x, factor_one, preferred_element_type=jnp.float32).astype(jnp.bfloat16)
    square_two = jnp.dot(next_x, next_x[:, :B], preferred_element_type=jnp.float32)
    factor_two = (1.5 * identity[:, :B] - 0.5 * square_two).astype(jnp.bfloat16)
    final_x = jnp.dot(next_x, factor_two, preferred_element_type=jnp.float32)
    return (0.5 * (identity[:, :B] - final_x)).astype(jnp.bfloat16)

def reference(block_store, block_source, chem_pot, basis_values, core_density, point_weights, pair_dest, tile_pairs):
    chem = chem_pot[0]
    flat_source = block_source.reshape(N_ATOMS * N_SPACE, SLOTS)
    space_index = (jnp.arange(N_ATOMS * N_SPACE) % N_SPACE).astype(jnp.int32)

    def one_device(items):
        source, space_at = items
        row_store = jnp.take(block_store, space_at, axis=0)
        blocks = jnp.take(row_store, source, axis=0)
        return sign_density(blocks, chem)
    density = lax.map(one_device, (flat_source, space_index)).reshape(N_ATOMS, N_SPACE, M, B)

    def tile_group(items):
        columns, tables, cores, weights, destinations, slot_tables = items
        order = jnp.arange(SENDS)
        earlier = (destinations[:, :, None] == destinations[:, None, :]) & (order[None, None, :] < order[None, :, None])
        arrival = lax.optimization_barrier(jnp.sum(earlier.astype(jnp.int32), axis=2)).astype(jnp.int32)
        slot_at = (jnp.arange(N_SPACE)[:, None] * CAPT + arrival).astype(jnp.int32)
        row_blocks = slot_tables[destinations, 0, slot_at].reshape(-1)
        col_blocks = slot_tables[destinations, 1, slot_at].reshape(-1)
        dest_flat = destinations.reshape(-1)
        left_basis = tables[dest_flat, row_blocks].astype(jnp.float32)
        right_basis = tables[dest_flat, col_blocks].astype(jnp.float32)
        pair_blocks = columns.reshape(N_SPACE, KB, B, B)[:, order // 2].reshape(-1, B, B)
        product = jnp.einsum('nij,njp->nip', pair_blocks.astype(jnp.float32), right_basis)
        terms = lax.optimization_barrier(jnp.sum(left_basis * product, axis=1))
        valence = jnp.zeros((N_SPACE, PTS), jnp.float32).at[dest_flat].add(terms)
        potential = -slater_factor * jnp.cbrt(jnp.maximum(cores + valence, density_floor))
        scaled = weights * potential
        weighted = (left_basis * scaled[dest_flat][:, None, :]).astype(jnp.bfloat16)
        partial_value = jnp.einsum('nip,njp->nij', weighted.astype(jnp.float32), right_basis).astype(jnp.bfloat16)
        kohn = partial_value.astype(jnp.float32).reshape(N_SPACE, KB, 2, B, B).sum(axis=2).reshape(N_SPACE, M, B)
        return (potential, kohn)
    potential, kohn_sham = lax.map(tile_group, (density, basis_values, core_density, point_weights, pair_dest, tile_pairs))
    return (density, potential, kohn_sham)
```

```python
import math

import jax
import jax.numpy as jnp
from jax import lax
from jax.experimental import pallas as pl
from jax.experimental.pallas import tpu as pltpu
from jax.sharding import PartitionSpec as P

RING = 8
CORES = 2
SPACE = RING * CORES
B = 128
H = B // 2
KB = 6
M = KB * B
SLOTS = KB * KB
SENDS = 2 * KB
NB = 4
NLOC = 8
PTS = 1024
SLATER = math.pow(3.0 / math.pi, 1.0 / 3.0)
FLOOR = 0.05
MESH = pl.DeviceIdType.MESH
GROUPS = ((0, 1), (1, 2), (3, 2), (5, 2), (7, 1))


def ring_offset(r):
    half = (r + 1) // 2
    return half - 2 * half * (r % 2)


def ring_rank(d):
    return jnp.where(d < RING // 2, 2 * d, 2 * (RING - d) - 1)


def kernel(
    store_ref,
    source_ref,
    chem_ref,
    basis_hbm,
    core_ref,
    weight_ref,
    dest_ref,
    pairs_ref,
    density_hbm,
    potential_ref,
    kohn_hbm,
    *scratch,
):
    held = (scratch[0:8], scratch[8:16])
    (
        want_out,
        want_in,
        want_sm,
        out0,
        out1,
        in0,
        in1,
        shifted,
        x_mat,
        t_mat,
        x1_mat,
        tables,
        density,
        pair_out,
        pair_in,
        part_out,
        part_in,
        kohn,
        local_sem,
        want_send,
        want_recv,
        ring_send,
        ring_recv,
        slot_send,
        slot_recv,
        pair_send,
        pair_recv,
        part_send,
        part_recv,
    ) = scratch[16:]
    outs, ins = (out0, out1), (in0, in1)
    atom, space = lax.axis_index("atoms"), lax.axis_index("space")
    y, z = atom // RING, atom % RING
    x, core = space // CORES, space % CORES
    me = (y, z)

    def across(h, at):
        return (at * RING + z, space) if h == 0 else (y * RING + at, space)

    def along(h, off):
        if h == 0:
            return (y * RING + (z + off) % RING, space)
        return (((y + off) % RING) * RING + z, space)

    barrier = pltpu.get_barrier_semaphore()
    for off in range(1, RING):
        for h in range(2):
            pl.semaphore_signal(barrier, inc=1, device_id=along(h, off), device_id_type=MESH)
    for off in range(1, SPACE):
        other = (atom, (space + off) % SPACE)
        pl.semaphore_signal(barrier, inc=1, device_id=other, device_id_type=MESH)

    basis_copy = pltpu.make_async_copy(basis_hbm, tables, local_sem.at[0])
    basis_copy.start()
    for h in range(2):
        held[h][0][...] = store_ref[:, h * H : (h + 1) * H, :]

    row = lax.broadcasted_iota(jnp.int32, (RING, B), 0)
    off = ring_offset(lax.broadcasted_iota(jnp.int32, (RING, B), 1))
    peer0 = row * RING + (z + off + RING * B) % RING
    peer1 = ((y + off + RING * B) % RING) * RING + row
    want0 = jnp.zeros((RING, B), jnp.int32)
    want1 = jnp.zeros((RING, B), jnp.int32)
    for m in range(SLOTS):
        number = source_ref[m]
        want0 = jnp.where(peer0 == number // NB, number % NB, want0)
        want1 = jnp.where(peer1 == number // NB, number % NB, want1)
    for h, want in enumerate((want0, want1)):
        want_out[h] = want
        want_in[h, me[h]] = want

    pl.semaphore_wait(barrier, 2 * (RING - 1) + SPACE - 1)

    def ring_copies(step):
        copies = []
        for h in range(2):
            for way in range(2):
                if step < 4:
                    src = held[h][0 if step == 1 else 2 * step - 3 + way]
                    dst = held[h][2 * step - 1 + way]
                else:
                    src = held[h][5 + way].at[pl.ds(2 * way, 2)]
                    dst = held[h][7].at[pl.ds(2 * way, 2)]
                copies.append(
                    pltpu.make_async_remote_copy(
                        src_ref=src,
                        dst_ref=dst,
                        send_sem=ring_send.at[h, way, step - 1],
                        recv_sem=ring_recv.at[h, way, step - 1],
                        device_id=along(h, 1 if way == 0 else RING - 1),
                        device_id_type=MESH,
                    )
                )
        return copies

    rings = [ring_copies(step) for step in range(1, 5)]
    for copy in rings[0]:
        copy.start()
    wants = []
    for h in range(2):
        for n in range(RING - 1, 0, -1):
            at = (me[h] + ring_offset(n) + RING) % RING
            wants.append(
                pltpu.make_async_remote_copy(
                    src_ref=want_out.at[h],
                    dst_ref=want_in.at[h, me[h]],
                    send_sem=want_send.at[h, n - 1],
                    recv_sem=want_recv.at[h, n - 1],
                    device_id=across(h, at),
                    device_id_type=MESH,
                )
            )
            wants[-1].start()
    for copy in wants:
        copy.wait()
    to_scalar = pltpu.make_async_copy(want_in, want_sm, local_sem.at[1])
    to_scalar.start()
    to_scalar.wait()

    def pick(h, at, first, count):
        for r in range(first, first + count):
            outs[h][at, r] = held[h][r][want_sm[h, at, me[h], r]]

    for group, (first, count) in enumerate(GROUPS):
        if group > 0:
            for copy in rings[group - 1]:
                copy.wait_recv()
        if 0 < group < 4:
            for copy in rings[group]:
                copy.start()

        def send_slots(i, carry, first=first, count=count):
            for h in range(2):
                at = (me[h] + ring_offset(RING - 1 - i) + RING) % RING
                pick(h, at, first, count)
                pltpu.make_async_remote_copy(
                    src_ref=outs[h].at[at, pl.ds(first, count)],
                    dst_ref=ins[h].at[me[h], pl.ds(first, count)],
                    send_sem=slot_send.at[h],
                    recv_sem=slot_recv.at[h],
                    device_id=across(h, at),
                    device_id_type=MESH,
                ).start()
            return carry

        lax.fori_loop(0, RING - 1, send_slots, 0)
        for h in range(2):
            for r in range(first, first + count):
                ins[h][me[h], r] = held[h][r][want_sm[h, me[h], me[h], r]]

    owner = []
    for n in range(SPACE):
        tile = ((x + ring_offset(n // CORES) + RING) % RING) * CORES + (core + n % CORES) % CORES
        block = 0
        for j in range(SENDS):
            block = jnp.where(dest_ref[j] == tile, j // 2, block)
        owner.append((tile, block))

    for h in range(2):
        most = ins[h].at[pl.ds(0, RING - 1)]
        pltpu.make_async_copy(most, most, slot_recv.at[h]).wait()

    eye = (
        lax.broadcasted_iota(jnp.int32, (B, B), 0) == lax.broadcasted_iota(jnp.int32, (B, B), 1)
    ).astype(jnp.float32)
    chem = chem_ref[0]

    def block(i, j):
        peer = source_ref[i * KB + j] // NB
        py, pz = peer // RING, peer % RING
        top = in0[py, ring_rank((pz - z + RING) % RING)]
        low = in1[pz, ring_rank((py - y + RING) % RING)]
        return jnp.concatenate([top, low], axis=0)

    upper = [(i, j) for i in range(KB) for j in range(i, KB)]
    total = jnp.zeros((8, B), jnp.float32)
    for n, (i, j) in enumerate(upper):
        here = block(i, j)
        there = here if i == j else block(j, i)
        value = 0.5 * (here.astype(jnp.float32) + there.T.astype(jnp.float32))
        if i == j:
            value = value - chem * eye
        shifted[n] = value
        square = jnp.sum((value * value).reshape(B // 8, 8, B), axis=0)
        total = total + (square if i == j else 2.0 * square)
    scale = 2.0 * jnp.sqrt(jnp.sum(total, keepdims=True) / M + 1e-06)
    factor = 1.0 / scale
    for n, (i, j) in enumerate(upper):
        value = (shifted[n] * factor).astype(jnp.bfloat16)
        x_mat[i * B : (i + 1) * B, j * B : (j + 1) * B] = value
        if i != j:
            x_mat[j * B : (j + 1) * B, i * B : (i + 1) * B] = value.T

    wide = 2 * B

    def identity(n):
        rows = lax.broadcasted_iota(jnp.int32, (M, wide), 0)
        columns = lax.broadcasted_iota(jnp.int32, (M, wide), 1) + n * wide
        return (rows == columns).astype(jnp.float32)

    for n in range(M // wide):
        at = slice(n * wide, (n + 1) * wide)
        square = jnp.dot(x_mat[...], x_mat[:, at], preferred_element_type=jnp.float32)
        t_mat[:, at] = (1.5 * identity(n) - 0.5 * square).astype(jnp.bfloat16)
    for n in range(M // wide):
        at = slice(n * wide, (n + 1) * wide)
        x1_mat[:, at] = jnp.dot(
            x_mat[...], t_mat[:, at], preferred_element_type=jnp.float32
        ).astype(jnp.bfloat16)
    first_columns = identity(0)[:, :B]
    square = jnp.dot(x1_mat[...], x1_mat[:, :B], preferred_element_type=jnp.float32)
    t2 = (1.5 * first_columns - 0.5 * square).astype(jnp.bfloat16)
    final = jnp.dot(x1_mat[...], t2, preferred_element_type=jnp.float32)
    density[...] = (0.5 * (first_columns - final)).astype(jnp.bfloat16).reshape(KB, B, B)
    density_copy = pltpu.make_async_copy(density, density_hbm, local_sem.at[2])
    density_copy.start()

    def mirror(n):
        rank, other = n // CORES, n % CORES
        if rank not in (0, RING - 1):
            rank = rank + 1 if rank % 2 else rank - 1
        return rank * CORES + other

    pair_in[0] = density[owner[0][1]]
    pair_copies = []
    for n in range(SPACE - 1, 0, -1):
        tile, number = owner[n]
        pair_out[n] = density[number]
        pair_copies.append(
            pltpu.make_async_remote_copy(
                src_ref=pair_out.at[n],
                dst_ref=pair_in.at[mirror(n)],
                send_sem=pair_send.at[n],
                recv_sem=pair_recv.at[mirror(n)],
                device_id=(atom, tile),
                device_id_type=MESH,
            )
        )
        pair_copies[-1].start()
    basis_copy.wait()

    def place(n):
        at = (x + ring_offset(n // CORES) + RING) % RING
        return at * CORES + (core + n) % CORES

    def values_of(n, row_col):
        return pairs_ref[row_col, place(n)]

    def add_pair(n, valence):
        def arrived():
            pltpu.make_async_copy(pair_in.at[n], pair_in.at[n], pair_recv.at[n]).wait()

        pl.when(n > 0)(arrived)
        left, right = values_of(n, 0), values_of(n, 1)
        product = jnp.dot(
            pair_in[n], tables[jnp.maximum(right, 0)], preferred_element_type=jnp.float32
        )
        term = tables[jnp.maximum(left, 0)].astype(jnp.float32) * product
        term = jnp.sum(term.reshape(B // 8, 8, PTS), axis=0)
        return valence + jnp.where(left >= 0, term, 0.0)

    valence = lax.fori_loop(0, SPACE, add_pair, jnp.zeros((8, PTS), jnp.float32))
    valence = jnp.sum(valence, axis=0, keepdims=True)
    charge = jnp.maximum(core_ref[...] + valence, FLOOR)
    potential = -SLATER * jnp.exp(jnp.log(charge) * (1.0 / 3.0))
    potential_ref[...] = potential
    scaled = weight_ref[...] * potential

    def project(i, carry):
        n = SPACE - 1 - i
        left, right = values_of(n, 0), values_of(n, 1)
        weighted = tables[jnp.maximum(left, 0)].astype(jnp.float32) * scaled
        value = lax.dot_general(
            weighted.astype(jnp.bfloat16),
            tables[jnp.maximum(right, 0)],
            (((1,), (1,)), ((), ())),
            preferred_element_type=jnp.float32,
        ).astype(jnp.bfloat16)
        part_out[n] = value

        def send():
            pltpu.make_async_remote_copy(
                src_ref=part_out.at[n],
                dst_ref=part_in.at[space],
                send_sem=part_send,
                recv_sem=part_recv,
                device_id=(atom, place(n)),
                device_id_type=MESH,
            ).start()

        def keep():
            part_in[space] = value

        pl.when(n > 0)(send)
        pl.when(n == 0)(keep)
        return carry

    lax.fori_loop(0, SPACE, project, 0)
    most = part_in.at[pl.ds(0, SPACE - 1)]
    pltpu.make_async_copy(most, most, part_recv).wait()
    kohn_copies = []
    for k in range(KB):
        one, two = part_in[dest_ref[2 * k]], part_in[dest_ref[2 * k + 1]]
        kohn[k] = one.astype(jnp.float32) + two.astype(jnp.float32)
        kohn_copies.append(pltpu.make_async_copy(kohn.at[k], kohn_hbm.at[k], local_sem.at[3 + k]))
        kohn_copies[-1].start()

    for step in rings:
        for copy in step:
            copy.wait_send()
    for h in range(2):
        most = outs[h].at[pl.ds(0, RING - 1)]
        pltpu.make_async_copy(most, most, slot_send.at[h]).wait()
    for copy in pair_copies:
        copy.wait_send()
    most = part_out.at[pl.ds(1, SPACE - 1)]
    pltpu.make_async_copy(most, most, part_send).wait()
    density_copy.wait()
    for copy in kohn_copies:
        copy.wait()


def per_device(
    block_store,
    block_source,
    chem_pot,
    basis_values,
    core_density,
    point_weights,
    pair_dest,
    tile_pairs,
):
    bf16, f32 = jnp.bfloat16, jnp.float32
    vmem = pl.BlockSpec(memory_space=pltpu.VMEM)
    smem = pl.BlockSpec(memory_space=pltpu.SMEM)
    hbm = pl.BlockSpec(memory_space=pl.ANY)
    dma = pltpu.SemaphoreType.DMA
    density, potential, kohn = pl.pallas_call(
        kernel,
        out_shape=(
            jax.ShapeDtypeStruct((KB, B, B), bf16),
            jax.ShapeDtypeStruct((1, PTS), f32),
            jax.ShapeDtypeStruct((KB, B, B), f32),
        ),
        in_specs=[vmem, smem, smem, hbm, vmem, vmem, smem, smem],
        out_specs=(hbm, vmem, hbm),
        scratch_shapes=[pltpu.VMEM((NB, H, B), bf16)] * 16
        + [
            pltpu.VMEM((2, RING, B), jnp.int32),
            pltpu.VMEM((2, RING, RING, B), jnp.int32),
            pltpu.SMEM((2, RING, RING, B), jnp.int32),
            pltpu.VMEM((RING, RING, H, B), bf16),
            pltpu.VMEM((RING, RING, H, B), bf16),
            pltpu.VMEM((RING, RING, H, B), bf16),
            pltpu.VMEM((RING, RING, H, B), bf16),
            pltpu.VMEM((KB * (KB + 1) // 2, B, B), f32),
            pltpu.VMEM((M, M), bf16),
            pltpu.VMEM((M, M), bf16),
            pltpu.VMEM((M, M), bf16),
            pltpu.VMEM((NLOC, B, PTS), bf16),
            pltpu.VMEM((KB, B, B), bf16),
            pltpu.VMEM((SPACE, B, B), bf16),
            pltpu.VMEM((SPACE, B, B), bf16),
            pltpu.VMEM((SPACE, B, B), bf16),
            pltpu.VMEM((SPACE, B, B), bf16),
            pltpu.VMEM((KB, B, B), f32),
            dma((3 + KB,)),
            dma((2, RING - 1)),
            dma((2, RING - 1)),
            dma((2, 2, 4)),
            dma((2, 2, 4)),
            dma((2,)),
            dma((2,)),
            dma((SPACE,)),
            dma((SPACE,)),
            dma,
            dma,
        ],
        compiler_params=pltpu.CompilerParams(
            collective_id=0, has_side_effects=True, vmem_limit_bytes=48 * 2**20
        ),
        name="grid_exchange",
    )(
        block_store[0],
        block_source[0, 0],
        chem_pot,
        basis_values[0, 0],
        core_density[0],
        point_weights[0],
        pair_dest[0, 0],
        tile_pairs[0, 0],
    )
    return (
        density.reshape(1, 1, M, B),
        potential[None],
        kohn.reshape(1, 1, M, B),
    )


def solution(mesh):
    placed = (
        P("space", "atoms", None, None),
        P("atoms", "space", None),
        P(),
        P("atoms", "space", None, None, None),
        P("atoms", "space", None),
        P("atoms", "space", None),
        P("atoms", "space", None),
        P("atoms", "space", None, None),
    )
    return jax.shard_map(
        per_device,
        mesh=mesh,
        in_specs=placed,
        out_specs=(
            P("atoms", "space", None, None),
            P("atoms", "space", None),
            P("atoms", "space", None, None),
        ),
        check_vma=False,
    )
```

```python
import math

import jax
import jax.numpy as jnp
from jax import lax
from jax.experimental import pallas as pl
from jax.experimental.pallas import tpu as pltpu
from jax.sharding import PartitionSpec as P

RING = 8
CORES = 2
SPACE = RING * CORES
B = 128
H = B // 2
KB = 6
M = KB * B
SLOTS = KB * KB
SENDS = 2 * KB
NB = 4
NLOC = 8
PTS = 1024
SLATER = math.pow(3.0 / math.pi, 1.0 / 3.0)
FLOOR = 0.05
MESH = pl.DeviceIdType.MESH
GROUPS = ((0, 3), (3, 2), (5, 3))


def ring_offset(r):
    half = (r + 1) // 2
    return half - 2 * half * (r % 2)


def ring_rank(d):
    return jnp.where(d < RING // 2, 2 * d, 2 * (RING - d) - 1)


def kernel(
    store_hbm,
    source_hbm,
    chem_ref,
    basis_hbm,
    core_hbm,
    weight_hbm,
    dest_hbm,
    pairs_hbm,
    density,
    potential_ref,
    kohn,
    *scratch,
):
    held = (scratch[0:8], scratch[8:16])
    (
        want_out,
        want_in,
        want_sm,
        out0,
        out1,
        in0,
        in1,
        shifted,
        x_mat,
        t_mat,
        x1_mat,
        tables,
        pair_out,
        pair_in,
        part_out,
        part_in,
        store_ref,
        source_ref,
        core_ref,
        weight_ref,
        dest_ref,
        pairs_ref,
        local_sem,
        want_send,
        want_recv,
        ring_send,
        ring_recv,
        slot_send,
        slot_recv,
        pair_send,
        pair_recv,
        part_send,
        part_recv,
    ) = scratch[16:]
    outs, ins = (out0, out1), (in0, in1)
    atom, space = lax.axis_index("atoms"), lax.axis_index("space")
    y, z = atom // RING, atom % RING
    x, core = space // CORES, space % CORES
    me = (y, z)

    def across(h, at):
        return (at * RING + z, space) if h == 0 else (y * RING + at, space)

    def along(h, off):
        if h == 0:
            return (y * RING + (z + off) % RING, space)
        return (((y + off) % RING) * RING + z, space)

    copies_in = []
    for n, (src, dst) in enumerate(
        (
            (source_hbm, source_ref),
            (store_hbm, store_ref),
            (dest_hbm, dest_ref),
            (pairs_hbm, pairs_ref),
            (core_hbm, core_ref),
            (weight_hbm, weight_ref),
            (basis_hbm, tables),
        )
    ):
        copies_in.append(pltpu.make_async_copy(src, dst, local_sem.at[n]))
        copies_in[-1].start()

    barrier = pltpu.get_barrier_semaphore()
    for off in range(1, RING):
        for h in range(2):
            pl.semaphore_signal(barrier, inc=1, device_id=along(h, off), device_id_type=MESH)
    for off in range(1, SPACE):
        other = (atom, (space + off) % SPACE)
        pl.semaphore_signal(barrier, inc=1, device_id=other, device_id_type=MESH)

    for copy in copies_in[:2]:
        copy.wait()
    for h in range(2):
        held[h][0][...] = store_ref[:, h * H : (h + 1) * H, :]

    row = lax.broadcasted_iota(jnp.int32, (RING, B), 0)
    off = ring_offset(lax.broadcasted_iota(jnp.int32, (RING, B), 1))
    peer0 = row * RING + (z + off + RING * B) % RING
    peer1 = ((y + off + RING * B) % RING) * RING + row
    want0 = jnp.zeros((RING, B), jnp.int32)
    want1 = jnp.zeros((RING, B), jnp.int32)
    for m in range(SLOTS):
        number = source_ref[m]
        want0 = jnp.where(peer0 == number // NB, number % NB, want0)
        want1 = jnp.where(peer1 == number // NB, number % NB, want1)
    for h, want in enumerate((want0, want1)):
        want_out[h] = want
        want_in[h, me[h]] = want

    pl.semaphore_wait(barrier, 2 * (RING - 1) + SPACE - 1)

    def ring_copies(step):
        copies = []
        for h in range(2):
            for way in range(2):
                if step < 4:
                    src = held[h][0 if step == 1 else 2 * step - 3 + way]
                    dst = held[h][2 * step - 1 + way]
                else:
                    src = held[h][5 + way].at[pl.ds(2 * way, 2)]
                    dst = held[h][7].at[pl.ds(2 * way, 2)]
                copies.append(
                    pltpu.make_async_remote_copy(
                        src_ref=src,
                        dst_ref=dst,
                        send_sem=ring_send.at[h, way, step - 1],
                        recv_sem=ring_recv.at[h, way, step - 1],
                        device_id=along(h, 1 if way == 0 else RING - 1),
                        device_id_type=MESH,
                    )
                )
        return copies

    rings = [ring_copies(step) for step in range(1, 5)]

    def ring_arrived(step):
        for copy in rings[step - 1]:
            copy.wait_recv()
        if step < 4:
            for copy in rings[step]:
                copy.start()

    for copy in rings[0]:
        copy.start()
    wants = []
    for h in range(2):
        for n in range(RING - 1, 0, -1):
            at = (me[h] + ring_offset(n) + RING) % RING
            wants.append(
                pltpu.make_async_remote_copy(
                    src_ref=want_out.at[h],
                    dst_ref=want_in.at[h, me[h]],
                    send_sem=want_send.at[h, n - 1],
                    recv_sem=want_recv.at[h, n - 1],
                    device_id=across(h, at),
                    device_id_type=MESH,
                )
            )
            wants[-1].start()
    ring_arrived(1)
    for copy in wants:
        copy.wait()
    to_scalar = pltpu.make_async_copy(want_in, want_sm, local_sem.at[7])
    to_scalar.start()
    to_scalar.wait()

    def pick(h, at, first, count):
        for r in range(first, first + count):
            outs[h][at, r] = held[h][r][want_sm[h, at, me[h], r]]

    for group, (first, count) in enumerate(GROUPS):
        for step in ((2,), (3, 4))[group - 1] if group > 0 else ():
            ring_arrived(step)

        def send_slots(i, carry, first=first, count=count):
            for h in range(2):
                at = (me[h] + ring_offset(RING - 1 - i) + RING) % RING
                pick(h, at, first, count)
                pltpu.make_async_remote_copy(
                    src_ref=outs[h].at[at, pl.ds(first, count)],
                    dst_ref=ins[h].at[me[h], pl.ds(first, count)],
                    send_sem=slot_send.at[h],
                    recv_sem=slot_recv.at[h],
                    device_id=across(h, at),
                    device_id_type=MESH,
                ).start()
            return carry

        lax.fori_loop(0, RING - 1, send_slots, 0)
        for h in range(2):
            for r in range(first, first + count):
                ins[h][me[h], r] = held[h][r][want_sm[h, me[h], me[h], r]]

    for copy in copies_in[2:]:
        copy.wait()
    owner = []
    for n in range(SPACE):
        tile = ((x + ring_offset(n // CORES) + RING) % RING) * CORES + (core + n % CORES) % CORES
        block = 0
        for j in range(SENDS):
            block = jnp.where(dest_ref[j] == tile, j // 2, block)
        owner.append((tile, block))

    for h in range(2):
        most = ins[h].at[pl.ds(0, RING - 1)]
        pltpu.make_async_copy(most, most, slot_recv.at[h]).wait()

    eye = (
        lax.broadcasted_iota(jnp.int32, (B, B), 0) == lax.broadcasted_iota(jnp.int32, (B, B), 1)
    ).astype(jnp.float32)
    chem = chem_ref[0]

    def block(i, j):
        peer = source_ref[i * KB + j] // NB
        py, pz = peer // RING, peer % RING
        top = in0[py, ring_rank((pz - z + RING) % RING)]
        low = in1[pz, ring_rank((py - y + RING) % RING)]
        return jnp.concatenate([top, low], axis=0)

    upper = [(i, j) for i in range(KB) for j in range(i, KB)]
    total = jnp.zeros((8, B), jnp.float32)
    for n, (i, j) in enumerate(upper):
        here = block(i, j)
        there = here if i == j else block(j, i)
        value = 0.5 * (here.astype(jnp.float32) + there.T.astype(jnp.float32))
        if i == j:
            value = value - chem * eye
        shifted[n] = value
        square = jnp.sum((value * value).reshape(B // 8, 8, B), axis=0)
        total = total + (square if i == j else 2.0 * square)
    scale = 2.0 * jnp.sqrt(jnp.sum(total, keepdims=True) / M + 1e-06)
    factor = 1.0 / scale
    for n, (i, j) in enumerate(upper):
        value = (shifted[n] * factor).astype(jnp.bfloat16)
        x_mat[i * B : (i + 1) * B, j * B : (j + 1) * B] = value
        if i != j:
            x_mat[j * B : (j + 1) * B, i * B : (i + 1) * B] = value.T

    wide = 2 * B

    def identity(n):
        rows = lax.broadcasted_iota(jnp.int32, (M, wide), 0)
        columns = lax.broadcasted_iota(jnp.int32, (M, wide), 1) + n * wide
        return (rows == columns).astype(jnp.float32)

    for n in range(M // wide):
        at = slice(n * wide, (n + 1) * wide)
        square = jnp.dot(x_mat[...], x_mat[:, at], preferred_element_type=jnp.float32)
        t_mat[:, at] = (1.5 * identity(n) - 0.5 * square).astype(jnp.bfloat16)
    for n in range(M // wide):
        at = slice(n * wide, (n + 1) * wide)
        x1_mat[:, at] = jnp.dot(
            x_mat[...], t_mat[:, at], preferred_element_type=jnp.float32
        ).astype(jnp.bfloat16)
    first_columns = identity(0)[:, :B]
    square = jnp.dot(x1_mat[...], x1_mat[:, :B], preferred_element_type=jnp.float32)
    t2 = (1.5 * first_columns - 0.5 * square).astype(jnp.bfloat16)
    final = jnp.dot(x1_mat[...], t2, preferred_element_type=jnp.float32)
    density[...] = (0.5 * (first_columns - final)).astype(jnp.bfloat16).reshape(KB, B, B)

    def mirror(n):
        rank, other = n // CORES, n % CORES
        if rank not in (0, RING - 1):
            rank = rank + 1 if rank % 2 else rank - 1
        return rank * CORES + other

    pair_in[0] = density[owner[0][1]]
    pair_copies = []
    for n in range(SPACE - 1, 0, -1):
        tile, number = owner[n]
        pair_out[n] = density[number]
        pair_copies.append(
            pltpu.make_async_remote_copy(
                src_ref=pair_out.at[n],
                dst_ref=pair_in.at[mirror(n)],
                send_sem=pair_send.at[n],
                recv_sem=pair_recv.at[mirror(n)],
                device_id=(atom, tile),
                device_id_type=MESH,
            )
        )
        pair_copies[-1].start()

    def place(n):
        at = (x + ring_offset(n // CORES) + RING) % RING
        return at * CORES + (core + n) % CORES

    def values_of(n, row_col):
        return pairs_ref[row_col, place(n)]

    def add_pair(n, valence):
        def arrived():
            pltpu.make_async_copy(pair_in.at[n], pair_in.at[n], pair_recv.at[n]).wait()

        pl.when(n > 0)(arrived)
        left, right = values_of(n, 0), values_of(n, 1)
        product = jnp.dot(
            pair_in[n], tables[jnp.maximum(right, 0)], preferred_element_type=jnp.float32
        )
        term = tables[jnp.maximum(left, 0)].astype(jnp.float32) * product
        term = jnp.sum(term.reshape(B // 8, 8, PTS), axis=0)
        return valence + jnp.where(left >= 0, term, 0.0)

    valence = lax.fori_loop(0, SPACE, add_pair, jnp.zeros((8, PTS), jnp.float32))
    valence = jnp.sum(valence, axis=0, keepdims=True)
    charge = jnp.maximum(core_ref[...] + valence, FLOOR)
    potential = -SLATER * jnp.exp(jnp.log(charge) * (1.0 / 3.0))
    potential_ref[...] = potential
    scaled = weight_ref[...] * potential

    def project(i, carry):
        n = SPACE - 1 - i
        left, right = values_of(n, 0), values_of(n, 1)
        weighted = tables[jnp.maximum(left, 0)].astype(jnp.float32) * scaled
        value = lax.dot_general(
            weighted.astype(jnp.bfloat16),
            tables[jnp.maximum(right, 0)],
            (((1,), (1,)), ((), ())),
            preferred_element_type=jnp.float32,
        ).astype(jnp.bfloat16)
        part_out[n] = value

        def send():
            pltpu.make_async_remote_copy(
                src_ref=part_out.at[n],
                dst_ref=part_in.at[space],
                send_sem=part_send,
                recv_sem=part_recv,
                device_id=(atom, place(n)),
                device_id_type=MESH,
            ).start()

        def keep():
            part_in[space] = value

        pl.when(n > 0)(send)
        pl.when(n == 0)(keep)
        return carry

    lax.fori_loop(0, SPACE, project, 0)
    most = part_in.at[pl.ds(0, SPACE - 1)]
    pltpu.make_async_copy(most, most, part_recv).wait()
    for k in range(KB):
        one, two = part_in[dest_ref[2 * k]], part_in[dest_ref[2 * k + 1]]
        kohn[k] = one.astype(jnp.float32) + two.astype(jnp.float32)

    for step in rings:
        for copy in step:
            copy.wait_send()
    for h in range(2):
        most = outs[h].at[pl.ds(0, RING - 1)]
        pltpu.make_async_copy(most, most, slot_send.at[h]).wait()
    for copy in pair_copies:
        copy.wait_send()
    most = part_out.at[pl.ds(1, SPACE - 1)]
    pltpu.make_async_copy(most, most, part_send).wait()


def write_out(density, potential, kohn, density_hbm, potential_hbm, kohn_hbm, sems):
    copies = [
        pltpu.make_async_copy(density, density_hbm, sems.at[0]),
        pltpu.make_async_copy(potential, potential_hbm, sems.at[1]),
        pltpu.make_async_copy(kohn, kohn_hbm, sems.at[2]),
    ]
    for copy in copies:
        copy.start()
    for copy in copies:
        copy.wait()


def per_device(
    block_store,
    block_source,
    chem_pot,
    basis_values,
    core_density,
    point_weights,
    pair_dest,
    tile_pairs,
):
    bf16, f32 = jnp.bfloat16, jnp.float32
    vmem = pl.BlockSpec(memory_space=pltpu.VMEM)
    smem = pl.BlockSpec(memory_space=pltpu.SMEM)
    hbm = pl.BlockSpec(memory_space=pltpu.HBM)
    dma = pltpu.SemaphoreType.DMA
    density, potential, kohn = pl.pallas_call(
        kernel,
        out_shape=(
            jax.ShapeDtypeStruct((KB, B, B), bf16),
            jax.ShapeDtypeStruct((1, PTS), f32),
            jax.ShapeDtypeStruct((KB, B, B), f32),
        ),
        in_specs=[hbm, hbm, smem, hbm, hbm, hbm, hbm, hbm],
        out_specs=(vmem, vmem, vmem),
        scratch_shapes=[pltpu.VMEM((NB, H, B), bf16)] * 16
        + [
            pltpu.VMEM((2, RING, B), jnp.int32),
            pltpu.VMEM((2, RING, RING, B), jnp.int32),
            pltpu.SMEM((2, RING, RING, B), jnp.int32),
            pltpu.VMEM((RING, RING, H, B), bf16),
            pltpu.VMEM((RING, RING, H, B), bf16),
            pltpu.VMEM((RING, RING, H, B), bf16),
            pltpu.VMEM((RING, RING, H, B), bf16),
            pltpu.VMEM((KB * (KB + 1) // 2, B, B), f32),
            pltpu.VMEM((M, M), bf16),
            pltpu.VMEM((M, M), bf16),
            pltpu.VMEM((M, M), bf16),
            pltpu.VMEM((NLOC, B, PTS), bf16),
            pltpu.VMEM((SPACE, B, B), bf16),
            pltpu.VMEM((SPACE, B, B), bf16),
            pltpu.VMEM((SPACE, B, B), bf16),
            pltpu.VMEM((SPACE, B, B), bf16),
            pltpu.VMEM((NB, B, B), bf16),
            pltpu.SMEM((SLOTS,), jnp.int32),
            pltpu.VMEM((1, PTS), f32),
            pltpu.VMEM((1, PTS), f32),
            pltpu.SMEM((SENDS,), jnp.int32),
            pltpu.SMEM((2, SPACE), jnp.int32),
            dma((8,)),
            dma((2, RING - 1)),
            dma((2, RING - 1)),
            dma((2, 2, 4)),
            dma((2, 2, 4)),
            dma((2,)),
            dma((2,)),
            dma((SPACE,)),
            dma((SPACE,)),
            dma,
            dma,
        ],
        compiler_params=pltpu.CompilerParams(
            collective_id=0, has_side_effects=True, vmem_limit_bytes=58000 * 2**10
        ),
        name="grid_exchange",
    )(
        block_store[0],
        block_source[0, 0],
        chem_pot,
        basis_values[0, 0],
        core_density[0],
        point_weights[0],
        pair_dest[0, 0],
        tile_pairs[0, 0],
    )
    density, potential, kohn = pl.pallas_call(
        write_out,
        out_shape=(
            jax.ShapeDtypeStruct((KB, B, B), bf16),
            jax.ShapeDtypeStruct((1, PTS), f32),
            jax.ShapeDtypeStruct((KB, B, B), f32),
        ),
        in_specs=[vmem] * 3,
        out_specs=(hbm, hbm, hbm),
        scratch_shapes=[dma((3,))],
        name="write_out",
    )(density, potential, kohn)
    return (
        density.reshape(1, 1, M, B),
        potential[None],
        kohn.reshape(1, 1, M, B),
    )


def solution(mesh):
    placed = (
        P("space", "atoms", None, None),
        P("atoms", "space", None),
        P(),
        P("atoms", "space", None, None, None),
        P("atoms", "space", None),
        P("atoms", "space", None),
        P("atoms", "space", None),
        P("atoms", "space", None, None),
    )
    return jax.shard_map(
        per_device,
        mesh=mesh,
        in_specs=placed,
        out_specs=(
            P("atoms", "space", None, None),
            P("atoms", "space", None),
            P("atoms", "space", None, None),
        ),
        check_vma=False,
    )
```

```python
import math

import jax
import jax.numpy as jnp
from jax import lax
from jax.experimental import pallas as pl
from jax.experimental.pallas import tpu as pltpu
from jax.sharding import PartitionSpec as P

RING = 8
CORES = 2
SPACE = RING * CORES
B = 128
H = B // 2
KB = 6
M = KB * B
SLOTS = KB * KB
SENDS = 2 * KB
NB = 4
NLOC = 8
PTS = 1024
SLATER = math.pow(3.0 / math.pi, 1.0 / 3.0)
FLOOR = 0.05
MESH = pl.DeviceIdType.MESH
GROUPS = ((0, 3), (3, 2), (5, 3))


def ring_offset(r):
    half = (r + 1) // 2
    return half - 2 * half * (r % 2)


def ring_rank(d):
    return jnp.where(d < RING // 2, 2 * d, 2 * (RING - d) - 1)


def kernel(
    store_hbm,
    source_hbm,
    chem_ref,
    basis_hbm,
    core_hbm,
    weight_hbm,
    dest_hbm,
    pairs_hbm,
    density,
    potential_ref,
    kohn,
    *scratch,
):
    held = (scratch[0:8], scratch[8:16])
    (
        want_out,
        want_in,
        want_sm,
        out0,
        out1,
        in0,
        in1,
        shifted,
        x_mat,
        t_mat,
        x1_mat,
        tables,
        pair_out,
        pair_in,
        part_out,
        part_in,
        store_ref,
        source_ref,
        core_ref,
        weight_ref,
        dest_ref,
        pairs_ref,
        local_sem,
        want_send,
        want_recv,
        ring_send,
        ring_recv,
        slot_send,
        slot_recv,
        pair_send,
        pair_recv,
        part_send,
        part_recv,
    ) = scratch[16:]
    outs, ins = (out0, out1), (in0, in1)
    atom, space = lax.axis_index("atoms"), lax.axis_index("space")
    y, z = atom // RING, atom % RING
    x, core = space // CORES, space % CORES
    me = (y, z)

    def across(h, at):
        return (at * RING + z, space) if h == 0 else (y * RING + at, space)

    def along(h, off):
        if h == 0:
            return (y * RING + (z + off) % RING, space)
        return (((y + off) % RING) * RING + z, space)

    copies_in = []
    for n, (src, dst) in enumerate(
        (
            (source_hbm, source_ref),
            (store_hbm, store_ref),
            (dest_hbm, dest_ref),
            (pairs_hbm, pairs_ref),
            (core_hbm, core_ref),
            (weight_hbm, weight_ref),
            (basis_hbm, tables),
        )
    ):
        copies_in.append(pltpu.make_async_copy(src, dst, local_sem.at[n]))
        copies_in[-1].start()

    barrier = pltpu.get_barrier_semaphore()
    for off in range(1, RING):
        for h in range(2):
            pl.semaphore_signal(barrier, inc=1, device_id=along(h, off), device_id_type=MESH)
    for off in range(1, SPACE):
        other = (atom, (space + off) % SPACE)
        pl.semaphore_signal(barrier, inc=1, device_id=other, device_id_type=MESH)

    for copy in copies_in[:2]:
        copy.wait()
    for h in range(2):
        held[h][0][...] = store_ref[:, h * H : (h + 1) * H, :]

    row = lax.broadcasted_iota(jnp.int32, (RING, B), 0)
    off = ring_offset(lax.broadcasted_iota(jnp.int32, (RING, B), 1))
    peer0 = row * RING + (z + off + RING * B) % RING
    peer1 = ((y + off + RING * B) % RING) * RING + row
    want0 = jnp.zeros((RING, B), jnp.int32)
    want1 = jnp.zeros((RING, B), jnp.int32)
    for m in range(SLOTS):
        number = source_ref[m]
        want0 = jnp.where(peer0 == number // NB, number % NB, want0)
        want1 = jnp.where(peer1 == number // NB, number % NB, want1)
    for h, want in enumerate((want0, want1)):
        want_out[h] = want
        want_in[h, me[h]] = want

    pl.semaphore_wait(barrier, 2 * (RING - 1) + SPACE - 1)

    def ring_copies(step):
        copies = []
        for h in range(2):
            for way in range(2):
                if step < 4:
                    src = held[h][0 if step == 1 else 2 * step - 3 + way]
                    dst = held[h][2 * step - 1 + way]
                else:
                    src = held[h][5 + way].at[pl.ds(2 * way, 2)]
                    dst = held[h][7].at[pl.ds(2 * way, 2)]
                copies.append(
                    pltpu.make_async_remote_copy(
                        src_ref=src,
                        dst_ref=dst,
                        send_sem=ring_send.at[h, way, step - 1],
                        recv_sem=ring_recv.at[h, way, step - 1],
                        device_id=along(h, 1 if way == 0 else RING - 1),
                        device_id_type=MESH,
                    )
                )
        return copies

    rings = [ring_copies(step) for step in range(1, 5)]

    def ring_arrived(step):
        for copy in rings[step - 1]:
            copy.wait_recv()
        if step < 4:
            for copy in rings[step]:
                copy.start()

    for copy in rings[0]:
        copy.start()
    wants = []
    for h in range(2):
        for n in range(RING - 1, 0, -1):
            at = (me[h] + ring_offset(n) + RING) % RING
            wants.append(
                pltpu.make_async_remote_copy(
                    src_ref=want_out.at[h],
                    dst_ref=want_in.at[h, me[h]],
                    send_sem=want_send.at[h, n - 1],
                    recv_sem=want_recv.at[h, n - 1],
                    device_id=across(h, at),
                    device_id_type=MESH,
                )
            )
            wants[-1].start()
    ring_arrived(1)
    for copy in wants:
        copy.wait()
    to_scalar = pltpu.make_async_copy(want_in, want_sm, local_sem.at[7])
    to_scalar.start()
    to_scalar.wait()

    def pick(h, at, first, count):
        for r in range(first, first + count):
            outs[h][at, r] = held[h][r][want_sm[h, at, me[h], r]]

    for group, (first, count) in enumerate(GROUPS):
        for step in ((2,), (3, 4))[group - 1] if group > 0 else ():
            ring_arrived(step)

        def send_slots(i, carry, first=first, count=count):
            for h in range(2):
                at = (me[h] + ring_offset(RING - 1 - i) + RING) % RING
                pick(h, at, first, count)
                pltpu.make_async_remote_copy(
                    src_ref=outs[h].at[at, pl.ds(first, count)],
                    dst_ref=ins[h].at[me[h], pl.ds(first, count)],
                    send_sem=slot_send.at[h],
                    recv_sem=slot_recv.at[h],
                    device_id=across(h, at),
                    device_id_type=MESH,
                ).start()
            return carry

        lax.fori_loop(0, RING - 1, send_slots, 0)
        for h in range(2):
            for r in range(first, first + count):
                ins[h][me[h], r] = held[h][r][want_sm[h, me[h], me[h], r]]

    for copy in copies_in[2:]:
        copy.wait()
    owner = []
    for n in range(SPACE):
        tile = ((x + ring_offset(n // CORES) + RING) % RING) * CORES + (core + n % CORES) % CORES
        block = 0
        for j in range(SENDS):
            block = jnp.where(dest_ref[j] == tile, j // 2, block)
        owner.append((tile, block))

    for h in range(2):
        most = ins[h].at[pl.ds(0, RING - 1)]
        pltpu.make_async_copy(most, most, slot_recv.at[h]).wait()

    eye = (
        lax.broadcasted_iota(jnp.int32, (B, B), 0) == lax.broadcasted_iota(jnp.int32, (B, B), 1)
    ).astype(jnp.float32)
    chem = chem_ref[0]

    def block(i, j):
        peer = source_ref[i * KB + j] // NB
        py, pz = peer // RING, peer % RING
        top = in0[py, ring_rank((pz - z + RING) % RING)]
        low = in1[pz, ring_rank((py - y + RING) % RING)]
        return jnp.concatenate([top, low], axis=0)

    upper = [(i, j) for i in range(KB) for j in range(i, KB)]
    total = jnp.zeros((8, B), jnp.float32)
    for n, (i, j) in enumerate(upper):
        here = block(i, j)
        there = here if i == j else block(j, i)
        value = 0.5 * (here.astype(jnp.float32) + there.T.astype(jnp.float32))
        if i == j:
            value = value - chem * eye
        shifted[n] = value
        square = jnp.sum((value * value).reshape(B // 8, 8, B), axis=0)
        total = total + (square if i == j else 2.0 * square)
    scale = 2.0 * jnp.sqrt(jnp.sum(total, keepdims=True) / M + 1e-06)
    factor = 1.0 / scale
    for n, (i, j) in enumerate(upper):
        value = (shifted[n] * factor).astype(jnp.bfloat16)
        x_mat[i * B : (i + 1) * B, j * B : (j + 1) * B] = value
        if i != j:
            x_mat[j * B : (j + 1) * B, i * B : (i + 1) * B] = value.T

    wide = 2 * B

    def identity(n):
        rows = lax.broadcasted_iota(jnp.int32, (M, wide), 0)
        columns = lax.broadcasted_iota(jnp.int32, (M, wide), 1) + n * wide
        return (rows == columns).astype(jnp.float32)

    for n in range(M // wide):
        at = slice(n * wide, (n + 1) * wide)
        square = jnp.dot(x_mat[...], x_mat[:, at], preferred_element_type=jnp.float32)
        t_mat[:, at] = (1.5 * identity(n) - 0.5 * square).astype(jnp.bfloat16)
    for n in range(M // wide):
        at = slice(n * wide, (n + 1) * wide)
        x1_mat[:, at] = jnp.dot(
            x_mat[...], t_mat[:, at], preferred_element_type=jnp.float32
        ).astype(jnp.bfloat16)
    first_columns = identity(0)[:, :B]
    square = jnp.dot(x1_mat[...], x1_mat[:, :B], preferred_element_type=jnp.float32)
    t2 = (1.5 * first_columns - 0.5 * square).astype(jnp.bfloat16)
    final = jnp.dot(x1_mat[...], t2, preferred_element_type=jnp.float32)
    density[...] = (0.5 * (first_columns - final)).astype(jnp.bfloat16).reshape(KB, B, B)

    def mirror(n):
        rank, other = n // CORES, n % CORES
        if rank not in (0, RING - 1):
            rank = rank + 1 if rank % 2 else rank - 1
        return rank * CORES + other

    pair_in[0] = density[owner[0][1]]
    pair_copies = []
    for n in range(SPACE - 1, 0, -1):
        tile, number = owner[n]
        pair_out[n] = density[number]
        pair_copies.append(
            pltpu.make_async_remote_copy(
                src_ref=pair_out.at[n],
                dst_ref=pair_in.at[mirror(n)],
                send_sem=pair_send.at[n],
                recv_sem=pair_recv.at[mirror(n)],
                device_id=(atom, tile),
                device_id_type=MESH,
            )
        )
        pair_copies[-1].start()

    def place(n):
        at = (x + ring_offset(n // CORES) + RING) % RING
        return at * CORES + (core + n) % CORES

    def values_of(n, row_col):
        return pairs_ref[row_col, place(n)]

    def add_pair(n, valence):
        def arrived():
            pltpu.make_async_copy(pair_in.at[n], pair_in.at[n], pair_recv.at[n]).wait()

        pl.when(n > 0)(arrived)
        left, right = values_of(n, 0), values_of(n, 1)
        product = jnp.dot(
            pair_in[n], tables[jnp.maximum(right, 0)], preferred_element_type=jnp.float32
        )
        term = tables[jnp.maximum(left, 0)].astype(jnp.float32) * product
        term = jnp.sum(term.reshape(B // 8, 8, PTS), axis=0)
        return valence + jnp.where(left >= 0, term, 0.0)

    valence = lax.fori_loop(0, SPACE, add_pair, jnp.zeros((8, PTS), jnp.float32))
    valence = jnp.sum(valence, axis=0, keepdims=True)
    charge = jnp.maximum(core_ref[...] + valence, FLOOR)
    potential = -SLATER * jnp.exp(jnp.log(charge) * (1.0 / 3.0))
    potential_ref[...] = potential
    scaled = weight_ref[...] * potential

    def partial(n):
        left, right = values_of(n, 0), values_of(n, 1)
        weighted = tables[jnp.maximum(left, 0)].astype(jnp.float32) * scaled
        return lax.dot_general(
            weighted.astype(jnp.bfloat16),
            tables[jnp.maximum(right, 0)],
            (((1,), (1,)), ((), ())),
            preferred_element_type=jnp.float32,
        ).astype(jnp.bfloat16)

    def project(i, carry):
        places = [SPACE - 1 - 3 * i - k for k in range(3)]
        values = [partial(n) for n in places]
        for n, value in zip(places, values):
            part_out[n] = value
        for n in places:
            pltpu.make_async_remote_copy(
                src_ref=part_out.at[n],
                dst_ref=part_in.at[space],
                send_sem=part_send,
                recv_sem=part_recv,
                device_id=(atom, place(n)),
                device_id_type=MESH,
            ).start()
        return carry

    lax.fori_loop(0, (SPACE - 1) // 3, project, 0)
    part_in[space] = partial(0)
    most = part_in.at[pl.ds(0, SPACE - 1)]
    pltpu.make_async_copy(most, most, part_recv).wait()
    for k in range(KB):
        one, two = part_in[dest_ref[2 * k]], part_in[dest_ref[2 * k + 1]]
        kohn[k] = one.astype(jnp.float32) + two.astype(jnp.float32)

    for step in rings:
        for copy in step:
            copy.wait_send()
    for h in range(2):
        most = outs[h].at[pl.ds(0, RING - 1)]
        pltpu.make_async_copy(most, most, slot_send.at[h]).wait()
    for copy in pair_copies:
        copy.wait_send()
    most = part_out.at[pl.ds(1, SPACE - 1)]
    pltpu.make_async_copy(most, most, part_send).wait()


def write_out(density, potential, kohn, density_hbm, potential_hbm, kohn_hbm, sems):
    copies = [
        pltpu.make_async_copy(density, density_hbm, sems.at[0]),
        pltpu.make_async_copy(potential, potential_hbm, sems.at[1]),
        pltpu.make_async_copy(kohn, kohn_hbm, sems.at[2]),
    ]
    for copy in copies:
        copy.start()
    for copy in copies:
        copy.wait()


def per_device(
    block_store,
    block_source,
    chem_pot,
    basis_values,
    core_density,
    point_weights,
    pair_dest,
    tile_pairs,
):
    bf16, f32 = jnp.bfloat16, jnp.float32
    vmem = pl.BlockSpec(memory_space=pltpu.VMEM)
    smem = pl.BlockSpec(memory_space=pltpu.SMEM)
    hbm = pl.BlockSpec(memory_space=pltpu.HBM)
    dma = pltpu.SemaphoreType.DMA
    density, potential, kohn = pl.pallas_call(
        kernel,
        out_shape=(
            jax.ShapeDtypeStruct((KB, B, B), bf16),
            jax.ShapeDtypeStruct((1, PTS), f32),
            jax.ShapeDtypeStruct((KB, B, B), f32),
        ),
        in_specs=[hbm, hbm, smem, hbm, hbm, hbm, hbm, hbm],
        out_specs=(vmem, vmem, vmem),
        scratch_shapes=[pltpu.VMEM((NB, H, B), bf16)] * 16
        + [
            pltpu.VMEM((2, RING, B), jnp.int32),
            pltpu.VMEM((2, RING, RING, B), jnp.int32),
            pltpu.SMEM((2, RING, RING, B), jnp.int32),
            pltpu.VMEM((RING, RING, H, B), bf16),
            pltpu.VMEM((RING, RING, H, B), bf16),
            pltpu.VMEM((RING, RING, H, B), bf16),
            pltpu.VMEM((RING, RING, H, B), bf16),
            pltpu.VMEM((KB * (KB + 1) // 2, B, B), f32),
            pltpu.VMEM((M, M), bf16),
            pltpu.VMEM((M, M), bf16),
            pltpu.VMEM((M, M), bf16),
            pltpu.VMEM((NLOC, B, PTS), bf16),
            pltpu.VMEM((SPACE, B, B), bf16),
            pltpu.VMEM((SPACE, B, B), bf16),
            pltpu.VMEM((SPACE, B, B), bf16),
            pltpu.VMEM((SPACE, B, B), bf16),
            pltpu.VMEM((NB, B, B), bf16),
            pltpu.SMEM((SLOTS,), jnp.int32),
            pltpu.VMEM((1, PTS), f32),
            pltpu.VMEM((1, PTS), f32),
            pltpu.SMEM((SENDS,), jnp.int32),
            pltpu.SMEM((2, SPACE), jnp.int32),
            dma((8,)),
            dma((2, RING - 1)),
            dma((2, RING - 1)),
            dma((2, 2, 4)),
            dma((2, 2, 4)),
            dma((2,)),
            dma((2,)),
            dma((SPACE,)),
            dma((SPACE,)),
            dma,
            dma,
        ],
        compiler_params=pltpu.CompilerParams(
            collective_id=0, has_side_effects=True, vmem_limit_bytes=58000 * 2**10
        ),
        name="grid_exchange",
    )(
        block_store[0],
        block_source[0, 0],
        chem_pot,
        basis_values[0, 0],
        core_density[0],
        point_weights[0],
        pair_dest[0, 0],
        tile_pairs[0, 0],
    )
    density, potential, kohn = pl.pallas_call(
        write_out,
        out_shape=(
            jax.ShapeDtypeStruct((KB, B, B), bf16),
            jax.ShapeDtypeStruct((1, PTS), f32),
            jax.ShapeDtypeStruct((KB, B, B), f32),
        ),
        in_specs=[vmem] * 3,
        out_specs=(hbm, hbm, hbm),
        scratch_shapes=[dma((3,))],
        name="write_out",
    )(density, potential, kohn)
    return (
        density.reshape(1, 1, M, B),
        potential[None],
        kohn.reshape(1, 1, M, B),
    )


def solution(mesh):
    placed = (
        P("space", "atoms", None, None),
        P("atoms", "space", None),
        P(),
        P("atoms", "space", None, None, None),
        P("atoms", "space", None),
        P("atoms", "space", None),
        P("atoms", "space", None),
        P("atoms", "space", None, None),
    )
    return jax.shard_map(
        per_device,
        mesh=mesh,
        in_specs=placed,
        out_specs=(
            P("atoms", "space", None, None),
            P("atoms", "space", None),
            P("atoms", "space", None, None),
        ),
        check_vma=False,
    )
```
